32 devices in a mesh: groups: 2 (over x), attn: 8 (over z, y), exp: 2 (over core).
Axes of the slice: x: 2, y: 2, z: 4, core: 2. Of those that a mesh axis runs over, the one named last changes fastest.
Arguments:
- queries: bfloat16 [192, 6144], P(('groups', 'attn'), 'exp'), parts along dimension 0, may hold values from -6 to 6
- new_keys: bfloat16 [192, 1024], P(('groups', 'attn'), 'exp'), parts along dimension 0, may hold values from -6 to 6
- new_values: bfloat16 [192, 1024], P(('groups', 'attn'), 'exp'), parts along dimension 0, may hold values from -6 to 6
- key_cache: bfloat16 [192, 128, 1024], P(('groups', 'attn'), None, 'exp'), parts along dimension 0, may hold values from -6 to 6
- value_cache: bfloat16 [192, 128, 1024], P(('groups', 'attn'), None, 'exp'), parts along dimension 0, may hold values from -6 to 6
- cache_lengths: int32 [192], P(('groups', 'attn')), parts along dimension 0, may hold values from 1 to 128, as said below
- tokens: bfloat16 [192, 6144], P(('groups', 'attn')), parts along dimension 0, may hold values from -6 to 6
- expert_ids: int32 [192, 2], P(('groups', 'attn')), parts along dimension 0, may hold values from 0 to 3, all different within a row; in each aligned block of 12 rows (0 to 11, 12 to 23, ...) at most 8 rows name the same one
- gate_weights: float32 [192, 2], P(('groups', 'attn')), parts along dimension 0, may hold values from 0.2 to 1
- w_gate: bfloat16 [6144, 32768], P(None, ('attn', 'exp')), may hold values from -0.078125 to 0.078125
- w_up: bfloat16 [6144, 32768], P(None, ('attn', 'exp')), may hold values from -0.078125 to 0.078125
- w_down: bfloat16 [32768, 6144], P(('attn', 'exp')), may hold values from -0.0625 to 0.0625
Outputs:
- context: bfloat16 [192, 6144], P(('groups', 'attn'), 'exp'), parts along dimension 0
- expert_out: bfloat16 [192, 6144], P(('groups', 'attn')), parts along dimension 0
The draws below stay inside these ranges and needn't reach their ends.
There are 2 independent parts, one for each index of `groups`. The reference program is written for one: setup_inputs(seed, part) draws one part's arguments, and reference() takes and returns one part's arrays. A program takes and returns all parts, laid end to end along the dimension named above; an argument that names none is the same for every part. Nothing has to cross between parts.
Inputs may be any that keep to these rules, and one draw needn't show every extreme that they name: Each row attends to its first cache_lengths cached positions and to its new key. `expert_ids`: the two experts of a row differ; in the rows of one index of attn no expert is named more than 8 times, and that number is reached.
All inputs are finite; a program needn't handle non-finite values.
Results may differ from the reference program's by a relative error of at most 0.0058.
Values may be sent and summed in bfloat16 or wider, within the bound.
A program may use at most 192 MiB of HBM per device.

```python
import math
import jax
import jax.numpy as jnp
import numpy as np
from jax import lax

D = 6144
HEADS = 48
KV_HEADS = 8
HEAD_DIM = 128
EXPERTS = 4
FF = 8192
CACHE = 128
TOK_DEV = 12
CAPACITY = 8
ROWS = 96
N_ATTN = 8
N_EXP = 2


def draw_queries(key, part):
    key = jax.random.fold_in(key, 11)
    return jnp.clip(jax.random.normal(key, (ROWS, HEADS * HEAD_DIM), jnp.float32), -6.0, 6.0).astype(jnp.bfloat16)


def draw_key_cache(key, part):
    key = jax.random.fold_in(key, 13)
    return jnp.clip(jax.random.normal(key, (ROWS, CACHE, KV_HEADS * HEAD_DIM), jnp.float32), -6.0, 6.0).astype(jnp.bfloat16)


def draw_new_keys(key, part):
    key = jax.random.fold_in(key, 15)
    return jnp.clip(jax.random.normal(key, (ROWS, KV_HEADS * HEAD_DIM), jnp.float32), -6.0, 6.0).astype(jnp.bfloat16)


def draw_cache_lengths(key, part):
    key = jax.random.fold_in(key, 17)
    drawn = jax.random.randint(key, (ROWS,), 1, CACHE + 1, dtype=jnp.int32)
    return jnp.where(jnp.arange(ROWS) == 0, CACHE, drawn).astype(jnp.int32)


def levels(own_key, shape, cuts, least, largest):
    loudness, own = 1.0, jax.random.fold_in(own_key, 6)
    for dim, shards_of in cuts:
        steps = jnp.exp(jax.random.uniform(jax.random.fold_in(own, dim), (shards_of,), jnp.float32, least / len(cuts), largest / len(cuts)))
        loudness = loudness * jnp.repeat(steps, shape[dim] // shards_of).reshape([-1 if axis == dim else 1 for axis in range(len(shape))])
    return loudness


def deal_out(own_key, own, number, rows, amount, top, limit, slope):
    sequence = jax.random.permutation(own_key, amount)
    packed, common = load_shares(amount, rows * top, limit, slope, True), load_shares(amount, rows * top, limit, slope, False)
    places = jnp.arange(amount)

    def named(lengths, turn):
        used = int((lengths > 0).sum())
        fixed = max(1, used // 4)
        moved = fixed + (places - fixed + turn * (used - fixed)) % max(1, amount - fixed)
        return jnp.zeros((amount,), jnp.int32).at[sequence[jnp.where(places < fixed, places, moved)]].set(jnp.asarray(lengths, jnp.int32))

    lengths = jnp.where(number % 4 == 0, named(packed, number // 4), named(common, number - number // 4 - 1))
    mixed = jax.random.permutation(jax.random.fold_in(own, 3), amount)
    donor, receiver = mixed[0:amount // 2 * 2:2], mixed[1:amount // 2 * 2:2]
    margin = jnp.minimum(lengths[donor] - 1, limit - lengths[receiver]) // 2
    margin = jnp.where((donor == sequence[0]) | (receiver == sequence[0]) | (lengths[receiver] == 0), 0, jnp.maximum(margin, 0))
    moved = jax.random.randint(jax.random.fold_in(own, 4), (amount // 2,), 0, 1 << 20) % (margin + 1)
    lengths = lengths.at[donor].add(-moved).at[receiver].add(moved)
    members = jnp.searchsorted(jnp.cumsum(lengths), jnp.arange(rows * top), side="right").astype(jnp.int32)
    table = members.reshape(top, rows).T
    table = table[jax.random.permutation(jax.random.fold_in(own, 1), rows)]
    turn = jax.random.randint(jax.random.fold_in(own, 2), (rows, 1), 0, top)
    return jnp.take_along_axis(table, (jnp.arange(top)[None, :] + turn) % top, axis=1)


def load_shares(number_of, total, most, lean, full):
    portions = [(1 << 20) // math.isqrt(rank ** lean) + 1 for rank in range(1, number_of + 1)]
    largest = most if full else min(most, max(-(-total // number_of), total * portions[0] // sum(portions)))
    least = 1 if total - largest >= number_of - 1 else 0
    given, rest = [largest] + [least] * (number_of - 1), total - largest - least * (number_of - 1)
    while rest > 0:
        candidates = [i for i in range(1, number_of) if given[i] < largest] or [i for i in range(1, number_of) if given[i] < most]
        mass, remaining = sum([portions[i] for i in candidates]), rest
        for i in candidates:
            more = min(most - given[i], max(1, remaining * portions[i] // mass), rest)
            given[i] = given[i] + more
            rest = rest - more
    return np.array(given)


def normal_values(stream_key, extent, deviation, most, cuts=(), kind=jnp.bfloat16):
    gain = levels(stream_key, extent, cuts, -0.22, 0.18) if cuts else 1.0
    array = jax.random.normal(stream_key, extent, jnp.float32) * deviation * gain
    return jnp.minimum(jnp.maximum(array, -most), most).astype(kind)


def setup_inputs(seed: int = 0, part: int = 0) -> dict:
    seeds = jax.random.split(jax.random.key(seed), 13)
    part_splits = jax.random.split(jax.random.fold_in(seeds[12], part), 13)
    queries = draw_queries(jax.random.fold_in(jax.random.fold_in(seeds[12], part), 71), part)
    new_keys = draw_new_keys(jax.random.fold_in(jax.random.fold_in(seeds[12], part), 71), part)
    new_values = normal_values(part_splits[2], (ROWS, KV_HEADS * HEAD_DIM), 1.0, 6.0, ((0, 8), (1, 2)))
    key_cache = draw_key_cache(jax.random.fold_in(jax.random.fold_in(seeds[12], part), 71), part)
    value_cache = normal_values(part_splits[4], (ROWS, CACHE, KV_HEADS * HEAD_DIM), 1.0, 6.0, ((0, 8), (2, 2)))
    cache_lengths = draw_cache_lengths(jax.random.fold_in(jax.random.fold_in(seeds[12], part), 71), part)
    tokens = normal_values(part_splits[6], (ROWS, D), 1.0, 6.0, ((0, 8),))
    expert_ids_keys = jax.random.split(jax.random.fold_in(part_splits[7], 1), ROWS // TOK_DEV)
    expert_ids_turns = jax.random.permutation(jax.random.fold_in(part_splits[7], 3), ROWS // TOK_DEV)
    expert_ids = jax.vmap(lambda own, number: deal_out(jax.random.fold_in(part_splits[7], 2), own, number, TOK_DEV, EXPERTS, 2, CAPACITY, 2))(expert_ids_keys, expert_ids_turns).reshape((ROWS, 2))
    gate_weights = jnp.clip(0.2 + 0.8 * jax.random.uniform(part_splits[8], (ROWS, 2), jnp.float32) ** levels(part_splits[8], (ROWS, 2), ((0, 8),), -0.2, 0.2), 0.2, 1.0)
    w_gate = normal_values(seeds[9], (D, EXPERTS * FF), D ** -0.5, 0.078125, ((1, 16),))
    w_up = normal_values(seeds[10], (D, EXPERTS * FF), D ** -0.5, 0.078125, ((1, 16),))
    w_down = normal_values(seeds[11], (EXPERTS * FF, D), FF ** -0.5, 0.0625, ((0, 16),))
    return dict(queries=queries, new_keys=new_keys, new_values=new_values, key_cache=key_cache, value_cache=value_cache, cache_lengths=cache_lengths, tokens=tokens, expert_ids=expert_ids, gate_weights=gate_weights, w_gate=w_gate, w_up=w_up, w_down=w_down)


def attend(queries, new_keys, new_values, key_cache, value_cache, cache_lengths):
    row_count = queries.shape[0]
    shared = HEADS // KV_HEADS
    grouped = queries.astype(jnp.float32).reshape(row_count, KV_HEADS, shared, HEAD_DIM)
    key_heads = key_cache.astype(jnp.float32).reshape(row_count, CACHE, KV_HEADS, HEAD_DIM)
    value_heads = value_cache.astype(jnp.float32).reshape(row_count, CACHE, KV_HEADS, HEAD_DIM)
    own_keys = new_keys.astype(jnp.float32).reshape(row_count, KV_HEADS, HEAD_DIM)
    own_values = new_values.astype(jnp.float32).reshape(row_count, KV_HEADS, 1, HEAD_DIM)
    softmax_scale = HEAD_DIM ** -0.5
    cached = jnp.einsum("rgjd,rlgd->rgjl", grouped, key_heads, precision=lax.Precision.HIGHEST) * softmax_scale
    own_score = jnp.einsum("rgjd,rgd->rgj", grouped, own_keys, precision=lax.Precision.HIGHEST) * softmax_scale
    usable = jnp.arange(CACHE, dtype=jnp.int32)[None, None, None, :] < cache_lengths[:, None, None, None]
    cached = jnp.where(usable, cached, -1e30)
    highest = jnp.maximum(jnp.max(cached, axis=3), own_score)
    lifted = jnp.where(usable, jnp.exp(cached - highest[..., None]), 0.0)
    lifted_own = jnp.exp(own_score - highest)
    denominator = jnp.sum(lifted, axis=3) + lifted_own
    weights = (lifted / denominator[..., None]).astype(jnp.bfloat16)
    weight_own = (lifted_own / denominator).astype(jnp.bfloat16)
    mixed = jnp.einsum("rgjl,rlgd->rgjd", weights.astype(jnp.float32), value_heads, precision=lax.Precision.HIGHEST)
    mixed = mixed + weight_own[..., None].astype(jnp.float32) * own_values
    return mixed.reshape(row_count, HEADS * HEAD_DIM).astype(jnp.bfloat16)


def route_slots(expert_ids, block, count):
    row_count = expert_ids.shape[0]
    matches = (expert_ids[:, :, None] == jnp.arange(count, dtype=jnp.int32)[None, None, :]).astype(jnp.int32)
    per_row = jnp.sum(matches, axis=1).reshape(row_count // block, block, count)
    before = (jnp.cumsum(per_row, axis=1) - per_row).reshape(row_count, count)
    return jnp.sum(matches * before[:, None, :], axis=2).astype(jnp.int32)


def reference(queries, new_keys, new_values, key_cache, value_cache, cache_lengths, tokens, expert_ids, gate_weights, w_gate, w_up, w_down):
    context = attend(queries, new_keys, new_values, key_cache, value_cache, cache_lengths)
    row_count = tokens.shape[0]
    slot_pos = route_slots(expert_ids, TOK_DEV, EXPERTS)
    source = (jnp.arange(row_count, dtype=jnp.int32) // TOK_DEV)[:, None]
    target = ((expert_ids * N_ATTN + source) * CAPACITY + slot_pos).astype(jnp.int32)
    buffer = jnp.zeros((EXPERTS * N_ATTN * CAPACITY, D), jnp.bfloat16)
    buffer = buffer.at[target.reshape(-1)].set(jnp.repeat(tokens, 2, axis=0))
    group_count = N_ATTN // EXPERTS
    width_group = N_EXP * (EXPERTS * FF // (N_ATTN * N_EXP))
    slab = N_ATTN * CAPACITY
    outputs = []
    for expert in range(EXPERTS):
        expert_rows = buffer[expert * slab:(expert + 1) * slab]

        def add_group(carry, group):
            start = ((expert * group_count + group) * width_group).astype(jnp.int32)
            gate_cols = lax.dynamic_slice_in_dim(w_gate, start, width_group, 1)
            up_cols = lax.dynamic_slice_in_dim(w_up, start, width_group, 1)
            down_rows = lax.dynamic_slice_in_dim(w_down, start, width_group, 0)
            gate_pre = jnp.dot(expert_rows, gate_cols, preferred_element_type=jnp.float32)
            up_pre = jnp.dot(expert_rows, up_cols, preferred_element_type=jnp.float32)
            hidden = (jax.nn.silu(gate_pre) * up_pre).astype(jnp.bfloat16)
            term = jnp.dot(hidden, down_rows, preferred_element_type=jnp.float32).astype(jnp.bfloat16)
            term = lax.optimization_barrier(term)
            return carry + term.astype(jnp.float32), None

        summed, _ = lax.scan(add_group, jnp.zeros((slab, D), jnp.float32), jnp.arange(group_count, dtype=jnp.int32))
        outputs.append(summed)
    flat_all = jnp.stack(outputs).reshape(EXPERTS * slab, D)
    picked = flat_all[target]
    mixed = jnp.sum(gate_weights[:, :, None].astype(jnp.float32) * picked, axis=1)
    return context, mixed.astype(jnp.bfloat16)
```

```python
import functools

import jax
import jax.numpy as jnp
from jax import lax
from jax.experimental import pallas as pl
from jax.experimental.pallas import tpu as pltpu
from jax.sharding import PartitionSpec as P

HEAD_DIM = 128
EXPERTS = 4
CAPACITY = 8
MESH = pl.DeviceIdType.MESH
RING = 18
TILE = 512
DEPTH = 2048


def attend(queries, new_keys, new_values, key_cache, value_cache, cache_lengths):
    row_count = queries.shape[0]
    cache_len = key_cache.shape[1]
    kv_groups = key_cache.shape[2] // HEAD_DIM
    shared = queries.shape[1] // (kv_groups * HEAD_DIM)
    grouped = queries.reshape(row_count, kv_groups, shared, HEAD_DIM)
    key_heads = key_cache.reshape(row_count, cache_len, kv_groups, HEAD_DIM)
    value_heads = value_cache.reshape(row_count, cache_len, kv_groups, HEAD_DIM)
    own_keys = new_keys.reshape(row_count, kv_groups, HEAD_DIM)
    own_values = new_values.reshape(row_count, kv_groups, 1, HEAD_DIM).astype(jnp.float32)
    softmax_scale = HEAD_DIM ** (-0.5)
    cached = (
        jnp.einsum("rgjd,rlgd->rgjl", grouped, key_heads, preferred_element_type=jnp.float32)
        * softmax_scale
    )
    own_score = (
        jnp.einsum("rgjd,rgd->rgj", grouped, own_keys, preferred_element_type=jnp.float32)
        * softmax_scale
    )
    usable = (
        jnp.arange(cache_len, dtype=jnp.int32)[None, None, None, :]
        < cache_lengths[:, None, None, None]
    )
    cached = jnp.where(usable, cached, -1e30)
    highest = jnp.maximum(jnp.max(cached, axis=3), own_score)
    lifted = jnp.where(usable, jnp.exp(cached - highest[..., None]), 0.0)
    lifted_own = jnp.exp(own_score - highest)
    denominator = jnp.sum(lifted, axis=3) + lifted_own
    weights = (lifted / denominator[..., None]).astype(jnp.bfloat16)
    weight_own = (lifted_own / denominator).astype(jnp.bfloat16)
    mixed = jnp.einsum("rgjl,rlgd->rgjd", weights, value_heads, preferred_element_type=jnp.float32)
    mixed = mixed + weight_own[..., None].astype(jnp.float32) * own_values
    return mixed.reshape(row_count, kv_groups * shared * HEAD_DIM).astype(jnp.bfloat16)


def route_slots(expert_ids, block, count):
    row_count = expert_ids.shape[0]
    matches = (expert_ids[:, :, None] == jnp.arange(count, dtype=jnp.int32)[None, None, :]).astype(
        jnp.int32
    )
    per_row = jnp.sum(matches, axis=1).reshape(row_count // block, block, count)
    before = (jnp.cumsum(per_row, axis=1) - per_row).reshape(row_count, count)
    return jnp.sum(matches * before[:, None, :], axis=2)


def per_device(
    queries,
    new_keys,
    new_values,
    key_cache,
    value_cache,
    cache_lengths,
    tokens,
    expert_ids,
    gate_weights,
    w_gate,
    w_up,
    w_down,
):
    context = attend(queries, new_keys, new_values, key_cache, value_cache, cache_lengths)
    row_count, model_width = tokens.shape
    slot_pos = route_slots(expert_ids, row_count, EXPERTS)
    slot_index = expert_ids * CAPACITY + slot_pos
    targets = jnp.arange(EXPERTS * CAPACITY, dtype=jnp.int32)
    matches = slot_index[:, :, None] == targets[None, None, :]
    selector = jnp.any(matches, axis=1).T.astype(jnp.bfloat16)
    outgoing = jnp.dot(selector, tokens, preferred_element_type=jnp.float32).astype(jnp.bfloat16)
    outgoing = outgoing.reshape(EXPERTS, CAPACITY, model_width)
    attn_devices = lax.axis_size("attn")
    core_count = lax.axis_size("exp")
    half_slots = CAPACITY // core_count
    fanned = jnp.repeat(outgoing, attn_devices // EXPERTS, axis=0)
    received = lax.all_to_all(fanned, "attn", split_axis=0, concat_axis=0, tiled=True)
    flat_rows = received.reshape(attn_devices * CAPACITY, model_width)
    gate_pre = jnp.dot(flat_rows, w_gate, preferred_element_type=jnp.float32)
    up_pre = jnp.dot(flat_rows, w_up, preferred_element_type=jnp.float32)
    hidden = (jax.nn.silu(gate_pre) * up_pre).astype(jnp.bfloat16)
    partial_out = jnp.dot(hidden, w_down, preferred_element_type=jnp.float32)
    partial_out = partial_out.reshape(attn_devices, core_count, half_slots, model_width)
    group_share = lax.psum_scatter(partial_out, "exp", scatter_dimension=1, tiled=True).astype(
        jnp.bfloat16
    )
    combiner = jnp.sum(gate_weights[:, :, None] * matches.astype(jnp.float32), axis=1)
    both = lax.all_gather(group_share, "exp", axis=1, tiled=True)
    outbound = both.reshape(attn_devices, CAPACITY, model_width)
    returned = lax.all_to_all(outbound, "attn", split_axis=0, concat_axis=0, tiled=True)
    summed = jnp.sum(
        returned.astype(jnp.float32).reshape(
            EXPERTS, attn_devices // EXPERTS, CAPACITY, model_width
        ),
        axis=1,
    )
    combined = jnp.dot(
        combiner, summed.reshape(EXPERTS * CAPACITY, model_width), precision=lax.Precision.HIGHEST
    )
    return (context, combined.astype(jnp.bfloat16))


def attention_rows(lengths, qs, nkf, nvf, keys, values, os, first, count):
    heads = qs.shape[1]
    width = keys.shape[2]
    kv = width // HEAD_DIM
    shared = heads // kv
    cached = keys.shape[1]
    scale = HEAD_DIM ** (-0.5)
    row_id = lax.broadcasted_iota(jnp.int32, (heads, HEAD_DIM), 0)
    mine = [(row_id >= g * shared) & (row_id < (g + 1) * shared) for g in range(kv)]
    lane = lax.broadcasted_iota(jnp.int32, (heads, cached), 1)

    def pick(parts):
        total = jnp.where(mine[0], parts[0], 0.0)
        for g in range(1, kv):
            total = jnp.where(mine[g], parts[g], total)
        return total

    for step in range(count):
        r = first + step
        q = qs[r]
        spread = jnp.concatenate([jnp.where(m, q, 0.0) for m in mine], axis=1).astype(jnp.bfloat16)
        s = lax.dot_general(
            spread, keys[r], (((1,), (1,)), ((), ())), preferred_element_type=jnp.float32
        ) * scale
        usable = lane < lengths[r]
        s = jnp.where(usable, s, -1e30)
        nk = nkf[pl.ds(r, 1), :]
        nv = nvf[pl.ds(r, 1), :]
        cut = [slice(g * HEAD_DIM, (g + 1) * HEAD_DIM) for g in range(kv)]
        own_key = pick([jnp.broadcast_to(nk[:, k], (heads, HEAD_DIM)) for k in cut])
        own_value = pick([jnp.broadcast_to(nv[:, k], (heads, HEAD_DIM)) for k in cut])
        own = jnp.sum(q * own_key, axis=1, keepdims=True) * scale
        highest = jnp.maximum(jnp.max(s, axis=1, keepdims=True), own)
        lifted = jnp.where(usable, jnp.exp(s - highest), 0.0)
        lifted_own = jnp.exp(own - highest)
        den = jnp.sum(lifted, axis=1, keepdims=True) + lifted_own
        w = (lifted / den).astype(jnp.bfloat16)
        w_own = (lifted_own / den).astype(jnp.bfloat16).astype(jnp.float32)
        o = jnp.dot(w, values[r], preferred_element_type=jnp.float32)
        os[r] = pick([o[:, k] for k in cut]) + w_own * own_value


def layer_kernel(
    attn_count,
    lengths,
    queries,
    new_keys,
    new_values,
    key_cache,
    value_cache,
    tokens,
    expert_ids,
    gate_weights,
    w_gate,
    w_up,
    w_down,
    context,
    expert_out,
    q_v, nk_v, nv_v, k_v, v_v, tok_v, ids_v, gw_v,
    qs, nkf, nvf, os, ctx_v,
    outbuf, near, far, x, hid, ring,
    psend, pgot, tf, tb, yb, zf, zb, home, comb_v, ob,
    in_sem, ring_sem, put_sem,
    d_s, d_r, fy_s, fy_r, fs_s, fs_r,
    p_s, p_r, y_s, y_r, h_s, h_r, o_s, o_r,
):
    group = attn_count // EXPERTS
    a = lax.axis_index("attn")
    c = lax.axis_index("exp")
    ex, j = a // group, a % group
    rows, width = tok_v.shape
    half = width // 2
    hidden = hid.shape[1]
    k_parts = width // DEPTH
    n_blocks = hidden // TILE
    out_blocks = half // TILE
    per_block = 2 * k_parts

    pairs = [
        (tokens, tok_v), (expert_ids, ids_v), (gate_weights, gw_v), (queries, q_v),
        (new_keys, nk_v), (new_values, nv_v), (key_cache, k_v), (value_cache, v_v),
    ]
    loads = [pltpu.make_async_copy(s, d, in_sem.at[n]) for n, (s, d) in enumerate(pairs)]
    for load in loads:
        load.start()

    def up_tile(n, k, w):
        t = n * per_block + k * 2 + w
        slot = t % RING
        source = w_up if w else w_gate
        return slot, pltpu.make_async_copy(
            source.at[pl.ds(k * DEPTH, DEPTH), pl.ds(pl.multiple_of(n * TILE, TILE), TILE)],
            ring.at[slot],
            ring_sem.at[slot],
        )

    def down_tile(i, own):
        t = n_blocks * per_block + i * 2 + own
        slot = t % RING
        side = c if own else 1 - c
        first = pl.multiple_of((side * out_blocks + i) * TILE, TILE)
        return slot, pltpu.make_async_copy(
            w_down.at[:, pl.ds(first, TILE)], ring.at[slot], ring_sem.at[slot]
        )

    ahead = RING // per_block

    def prefetch(n, carry):
        for k in range(k_parts):
            for w in range(2):
                up_tile(n, k, w)[1].start()
        return carry

    lax.fori_loop(0, ahead, prefetch, 0)

    z_peer = [((ex + d) % EXPERTS) * group + j for d in range(EXPERTS)]
    y_peer = [ex * group + (j + d) % group for d in range(group)]
    barrier = pltpu.get_barrier_semaphore()
    for peer in z_peer[1:] + y_peer[1:]:
        pl.semaphore_signal(barrier, inc=1, device_id={"attn": peer}, device_id_type=MESH)
    pl.semaphore_signal(barrier, inc=1, device_id={"exp": 1 - c}, device_id_type=MESH)

    for load in loads[:3]:
        load.wait()
    ids = ids_v[...]
    gates = gw_v[...]
    spots = EXPERTS * CAPACITY
    lane = lax.broadcasted_iota(jnp.int32, (rows, spots), 1)
    row_id = lax.broadcasted_iota(jnp.int32, (rows, spots), 0)
    lane_expert, lane_slot = lane // CAPACITY, lane % CAPACITY
    first = ids[:, 0:1] == lane_expert
    second = ids[:, 1:2] == lane_expert
    routed = jnp.where(first | second, 1, 0)
    before = jnp.zeros((rows, spots), jnp.int32)
    for r in range(rows - 1):
        before = before + jnp.where(row_id > r, routed[r : r + 1, :], 0)
    chosen = (routed > 0) & (before == lane_slot)
    comb_v[...] = jnp.where(chosen, jnp.where(first, gates[:, 0:1], gates[:, 1:2]), 0.0)
    selector = jnp.where(chosen, 1.0, 0.0).astype(jnp.bfloat16)
    mine = tok_v[:, pl.ds(pl.multiple_of(c * half, half), half)]
    outgoing = lax.dot_general(
        selector, mine, (((0,), (0,)), ((), ())), preferred_element_type=jnp.float32
    )
    outbuf[...] = outgoing.reshape(EXPERTS, CAPACITY, half).astype(jnp.bfloat16)
    pl.semaphore_wait(barrier, EXPERTS + group - 1)

    def remote(src, dst, s_sem, r_sem, device):
        return pltpu.make_async_remote_copy(
            src_ref=src, dst_ref=dst, send_sem=s_sem, recv_sem=r_sem,
            device_id=device, device_id_type=MESH,
        )

    sends = []
    for d in range(1, EXPERTS):
        e2 = (ex + d) % EXPERTS
        cp = remote(
            outbuf.at[e2], near.at[j * EXPERTS + ex], d_s.at[d], d_r.at[ex], {"attn": z_peer[d]}
        )
        cp.start()
        sends.append(cp)
    near[j * EXPERTS + ex] = outbuf[ex]

    for load in loads[3:]:
        load.wait()
    heads = qs.shape[1]
    for h in range(heads):
        qs[:, h, :] = q_v[:, h * HEAD_DIM : (h + 1) * HEAD_DIM].astype(jnp.float32)
    nkf[...] = nk_v[...].astype(jnp.float32)
    nvf[...] = nv_v[...].astype(jnp.float32)
    at_once = 4 if rows % 4 == 0 else 1

    def attend_some(n, carry):
        attention_rows(lengths, qs, nkf, nvf, k_v, v_v, os, n * at_once, at_once)
        return carry

    def pass_on(place, e, direct):
        if direct:
            for d in range(1, group):
                cp = remote(
                    near.at[place], near.at[place], fy_s.at[e, d], fy_r.at[place],
                    {"attn": y_peer[d]},
                )
                cp.start()
                sends.append(cp)
        cp = remote(near.at[place], far.at[place], fs_s.at[place], fs_r.at[place], {"exp": 1 - c})
        cp.start()
        sends.append(cp)

    pass_on(j * EXPERTS + ex, ex, True)
    lax.fori_loop(0, rows // at_once, attend_some, 0)
    for d in range(1, EXPERTS):
        e2 = (ex + EXPERTS - d) % EXPERTS
        place = j * EXPERTS + e2
        remote(near.at[place], near.at[place], d_s.at[d], d_r.at[e2], {"exp": 1 - c}).wait_recv()
        pass_on(place, e2, True)
    for h in range(heads):
        ctx_v[:, h * HEAD_DIM : (h + 1) * HEAD_DIM] = os[:, h, :].astype(jnp.bfloat16)
    put_context = pltpu.make_async_copy(ctx_v, context, put_sem.at[0])
    put_context.start()
    for m in range(1, group):
        j2 = (j + m) % group
        for d in range(EXPERTS):
            e2 = (ex + EXPERTS - d) % EXPERTS
            place = j2 * EXPERTS + e2
            remote(
                near.at[place], near.at[place], fy_s.at[e2, m], fy_r.at[place], {"exp": 1 - c}
            ).wait_recv()
            pass_on(place, e2, False)
    for place in range(attn_count):
        remote(
            near.at[place], far.at[place], fs_s.at[place], fs_r.at[place], {"exp": 1 - c}
        ).wait_recv()
    slots = attn_count * CAPACITY
    x[:, pl.ds(pl.multiple_of(c * half, half), half)] = (
        near[...].astype(jnp.float32).reshape(slots, half).astype(jnp.bfloat16)
    )
    x[:, pl.ds(pl.multiple_of((1 - c) * half, half), half)] = (
        far[...].astype(jnp.float32).reshape(slots, half).astype(jnp.bfloat16)
    )

    def hidden_block(n, carry):
        sums = [None, None]
        for k in range(k_parts):
            for w in range(2):
                slot, tile = up_tile(n, k, w)
                tile.wait()
                term = jnp.dot(
                    x[:, k * DEPTH : (k + 1) * DEPTH], ring[slot],
                    preferred_element_type=jnp.float32,
                )
                sums[w] = term if k == 0 else sums[w] + term

                @pl.when(n + ahead < n_blocks)
                def _():
                    up_tile(n + ahead, k, w)[1].start()

                later = (n + ahead - n_blocks) * k_parts + k

                @pl.when((n + ahead >= n_blocks) & (later < out_blocks))
                def _():
                    down_tile(later, w)[1].start()

        g, u = sums
        act = g / (1.0 + jnp.exp(-g)) * u
        hid[:, pl.ds(pl.multiple_of(n * TILE, TILE), TILE)] = act.astype(jnp.bfloat16)
        return carry

    lax.fori_loop(0, n_blocks, hidden_block, 0)

    def sibling(i):
        return remote(psend.at[i], pgot.at[i], p_s.at[i], p_r.at[i], {"exp": 1 - c})

    def across(i, d):
        j2 = (j + d) % group
        return remote(tb.at[i, j2], yb.at[i, j], y_s.at[i, d], y_r.at[i, j], {"attn": y_peer[d]})

    def to_home(i, d):
        e2 = (ex + d) % EXPERTS
        return remote(zb.at[i, e2], home.at[i, ex], h_s.at[i, d], h_r.at[i, ex], {"attn": z_peer[d]})

    def finish(i):
        total = zf[i]
        for d in range(1, group):
            j2 = (j + d) % group
            remote(
                tb.at[i, j2], yb.at[i, j2], y_s.at[i, d], y_r.at[i, j2], {"exp": 1 - c}
            ).wait_recv()
            total = total + yb[i, j2].astype(jnp.float32).reshape(EXPERTS * CAPACITY, TILE)
        zb[i] = total.reshape(EXPERTS, CAPACITY, TILE).astype(jnp.bfloat16)
        for d in range(1, EXPERTS):
            to_home(i, d).start()
        home[i, ex] = zb[i, ex]

    def down_block(i, carry):
        slot, tile = down_tile(i, 0)
        tile.wait()
        psend[i] = jnp.dot(hid[...], ring[slot], preferred_element_type=jnp.float32)
        sibling(i).start()
        slot, tile = down_tile(i, 1)
        tile.wait()
        mine = jnp.dot(hid[...], ring[slot], preferred_element_type=jnp.float32)

        @pl.when(i > 0)
        def _():
            finish(i - 1)

        sibling(i).wait_recv()
        mine = mine + pgot[i]
        tf[...] = mine.reshape(group, EXPERTS * CAPACITY, TILE)
        tb[i] = mine.reshape(group, EXPERTS, CAPACITY, TILE).astype(jnp.bfloat16)
        zf[i] = tf[j]
        for d in range(1, group):
            across(i, d).start()
        return carry

    lax.fori_loop(0, out_blocks, down_block, 0)
    finish(out_blocks - 1)

    def combine(i, carry):
        for d in range(1, EXPERTS):
            e2 = (ex + d) % EXPERTS
            remote(
                zb.at[i, e2], home.at[i, e2], h_s.at[i, d], h_r.at[i, e2], {"exp": 1 - c}
            ).wait_recv()
        ob[:, pl.ds(pl.multiple_of(i * TILE, TILE), TILE)] = jnp.dot(
            comb_v[...], home[i].astype(jnp.float32).reshape(spots, TILE),
            precision=lax.Precision.HIGHEST, preferred_element_type=jnp.float32,
        ).astype(jnp.bfloat16)
        return carry

    lax.fori_loop(0, out_blocks, combine, 0)
    own_columns = pl.ds(pl.multiple_of(c * half, half), half)
    give = remote(ob, expert_out.at[:, own_columns], o_s, o_r, {"exp": 1 - c})
    give.start()
    put_out = pltpu.make_async_copy(ob, expert_out.at[:, own_columns], put_sem.at[1])
    put_out.start()
    for cp in sends:
        cp.wait_send()

    def drain(i, carry):
        sibling(i).wait_send()
        for d in range(1, group):
            across(i, d).wait_send()
        for d in range(1, EXPERTS):
            to_home(i, d).wait_send()
        return carry

    lax.fori_loop(0, out_blocks, drain, 0)
    put_context.wait()
    put_out.wait()
    other_columns = pl.ds(pl.multiple_of((1 - c) * half, half), half)
    give.wait_send()
    remote(ob, expert_out.at[:, other_columns], o_s, o_r, {"exp": 1 - c}).wait_recv()


def fused(
    queries, new_keys, new_values, key_cache, value_cache, cache_lengths,
    tokens, expert_ids, gate_weights, w_gate, w_up, w_down,
):
    n = lax.axis_size("attn")
    group = n // EXPERTS
    rows, width = tokens.shape
    half = width // 2
    heads = queries.shape[1] // HEAD_DIM
    hidden = w_gate.shape[1]
    blocks = half // TILE
    slots = n * CAPACITY
    bf, f32 = jnp.bfloat16, jnp.float32
    vm, dma = pltpu.VMEM, pltpu.SemaphoreType.DMA
    anywhere = pl.BlockSpec(memory_space=pl.ANY)
    return pl.pallas_call(
        functools.partial(layer_kernel, n),
        out_shape=(
            jax.ShapeDtypeStruct(queries.shape, bf),
            jax.ShapeDtypeStruct(tokens.shape, bf),
        ),
        in_specs=[pl.BlockSpec(memory_space=pltpu.SMEM)] + [anywhere] * 11,
        out_specs=(anywhere, anywhere),
        scratch_shapes=[
            vm(queries.shape, bf), vm(new_keys.shape, bf), vm(new_values.shape, bf),
            vm(key_cache.shape, bf), vm(value_cache.shape, bf), vm(tokens.shape, bf),
            vm(expert_ids.shape, jnp.int32), vm(gate_weights.shape, f32),
            vm((rows, heads, HEAD_DIM), f32), vm(new_keys.shape, f32), vm(new_values.shape, f32),
            vm((rows, heads, HEAD_DIM), f32), vm(queries.shape, bf),
            vm((EXPERTS, CAPACITY, half), bf), vm((n, CAPACITY, half), bf),
            vm((n, CAPACITY, half), bf), vm((slots, width), bf), vm((slots, hidden), bf),
            vm((RING, DEPTH, TILE), bf),
            vm((blocks, slots, TILE), f32), vm((blocks, slots, TILE), f32),
            vm((group, EXPERTS * CAPACITY, TILE), f32),
            vm((blocks, group, EXPERTS, CAPACITY, TILE), bf),
            vm((blocks, group, EXPERTS, CAPACITY, TILE), bf),
            vm((blocks, EXPERTS * CAPACITY, TILE), f32),
            vm((blocks, EXPERTS, CAPACITY, TILE), bf), vm((blocks, EXPERTS, CAPACITY, TILE), bf),
            vm((rows, EXPERTS * CAPACITY), f32), vm((rows, half), bf),
            dma((8,)), dma((RING,)), dma((2,)),
            dma((EXPERTS,)), dma((EXPERTS,)), dma((EXPERTS, group)), dma((n,)), dma((n,)), dma((n,)),
            dma((blocks,)), dma((blocks,)), dma((blocks, group)), dma((blocks, group)),
            dma((blocks, EXPERTS)), dma((blocks, EXPERTS)), dma(()), dma(()),
        ],
        compiler_params=pltpu.CompilerParams(
            collective_id=0, has_side_effects=True, vmem_limit_bytes=60 * 1024 * 1024
        ),
        name="decode_layer",
    )(
        cache_lengths, queries, new_keys, new_values, key_cache, value_cache,
        tokens, expert_ids, gate_weights, w_gate, w_up, w_down,
    )


def fits(mesh):
    return mesh.shape["exp"] == 2 and mesh.shape["attn"] == 2 * EXPERTS


def solution(mesh):
    placed = (
        P(("groups", "attn"), "exp"),
        P(("groups", "attn"), "exp"),
        P(("groups", "attn"), "exp"),
        P(("groups", "attn"), None, "exp"),
        P(("groups", "attn"), None, "exp"),
        P(("groups", "attn")),
        P(("groups", "attn"), None),
        P(("groups", "attn"), None),
        P(("groups", "attn"), None),
        P(None, ("attn", "exp")),
        P(None, ("attn", "exp")),
        P(("attn", "exp"), None),
    )
    return jax.shard_map(
        fused if fits(mesh) else per_device,
        mesh=mesh,
        in_specs=placed,
        out_specs=(P(("groups", "attn"), "exp"), P(("groups", "attn"), None)),
        check_vma=False,
    )
```

```python
import functools

import jax
import jax.numpy as jnp
from jax import lax
from jax.experimental import pallas as pl
from jax.experimental.pallas import tpu as pltpu
from jax.sharding import PartitionSpec as P

HEAD_DIM = 128
EXPERTS = 4
CAPACITY = 8
MESH = pl.DeviceIdType.MESH
RING = 18
TILE = 512
DEPTH = 2048
LAG = 3


def attend(queries, new_keys, new_values, key_cache, value_cache, cache_lengths):
    row_count = queries.shape[0]
    cache_len = key_cache.shape[1]
    kv_groups = key_cache.shape[2] // HEAD_DIM
    shared = queries.shape[1] // (kv_groups * HEAD_DIM)
    grouped = queries.reshape(row_count, kv_groups, shared, HEAD_DIM)
    key_heads = key_cache.reshape(row_count, cache_len, kv_groups, HEAD_DIM)
    value_heads = value_cache.reshape(row_count, cache_len, kv_groups, HEAD_DIM)
    own_keys = new_keys.reshape(row_count, kv_groups, HEAD_DIM)
    own_values = new_values.reshape(row_count, kv_groups, 1, HEAD_DIM).astype(jnp.float32)
    softmax_scale = HEAD_DIM ** (-0.5)
    cached = (
        jnp.einsum("rgjd,rlgd->rgjl", grouped, key_heads, preferred_element_type=jnp.float32)
        * softmax_scale
    )
    own_score = (
        jnp.einsum("rgjd,rgd->rgj", grouped, own_keys, preferred_element_type=jnp.float32)
        * softmax_scale
    )
    usable = (
        jnp.arange(cache_len, dtype=jnp.int32)[None, None, None, :]
        < cache_lengths[:, None, None, None]
    )
    cached = jnp.where(usable, cached, -1e30)
    highest = jnp.maximum(jnp.max(cached, axis=3), own_score)
    lifted = jnp.where(usable, jnp.exp(cached - highest[..., None]), 0.0)
    lifted_own = jnp.exp(own_score - highest)
    denominator = jnp.sum(lifted, axis=3) + lifted_own
    weights = (lifted / denominator[..., None]).astype(jnp.bfloat16)
    weight_own = (lifted_own / denominator).astype(jnp.bfloat16)
    mixed = jnp.einsum("rgjl,rlgd->rgjd", weights, value_heads, preferred_element_type=jnp.float32)
    mixed = mixed + weight_own[..., None].astype(jnp.float32) * own_values
    return mixed.reshape(row_count, kv_groups * shared * HEAD_DIM).astype(jnp.bfloat16)


def route_slots(expert_ids, block, count):
    row_count = expert_ids.shape[0]
    matches = (expert_ids[:, :, None] == jnp.arange(count, dtype=jnp.int32)[None, None, :]).astype(
        jnp.int32
    )
    per_row = jnp.sum(matches, axis=1).reshape(row_count // block, block, count)
    before = (jnp.cumsum(per_row, axis=1) - per_row).reshape(row_count, count)
    return jnp.sum(matches * before[:, None, :], axis=2)


def per_device(
    queries,
    new_keys,
    new_values,
    key_cache,
    value_cache,
    cache_lengths,
    tokens,
    expert_ids,
    gate_weights,
    w_gate,
    w_up,
    w_down,
):
    context = attend(queries, new_keys, new_values, key_cache, value_cache, cache_lengths)
    row_count, model_width = tokens.shape
    slot_pos = route_slots(expert_ids, row_count, EXPERTS)
    slot_index = expert_ids * CAPACITY + slot_pos
    targets = jnp.arange(EXPERTS * CAPACITY, dtype=jnp.int32)
    matches = slot_index[:, :, None] == targets[None, None, :]
    selector = jnp.any(matches, axis=1).T.astype(jnp.bfloat16)
    outgoing = jnp.dot(selector, tokens, preferred_element_type=jnp.float32).astype(jnp.bfloat16)
    outgoing = outgoing.reshape(EXPERTS, CAPACITY, model_width)
    attn_devices = lax.axis_size("attn")
    core_count = lax.axis_size("exp")
    half_slots = CAPACITY // core_count
    fanned = jnp.repeat(outgoing, attn_devices // EXPERTS, axis=0)
    received = lax.all_to_all(fanned, "attn", split_axis=0, concat_axis=0, tiled=True)
    flat_rows = received.reshape(attn_devices * CAPACITY, model_width)
    gate_pre = jnp.dot(flat_rows, w_gate, preferred_element_type=jnp.float32)
    up_pre = jnp.dot(flat_rows, w_up, preferred_element_type=jnp.float32)
    hidden = (jax.nn.silu(gate_pre) * up_pre).astype(jnp.bfloat16)
    partial_out = jnp.dot(hidden, w_down, preferred_element_type=jnp.float32)
    partial_out = partial_out.reshape(attn_devices, core_count, half_slots, model_width)
    group_share = lax.psum_scatter(partial_out, "exp", scatter_dimension=1, tiled=True).astype(
        jnp.bfloat16
    )
    combiner = jnp.sum(gate_weights[:, :, None] * matches.astype(jnp.float32), axis=1)
    both = lax.all_gather(group_share, "exp", axis=1, tiled=True)
    outbound = both.reshape(attn_devices, CAPACITY, model_width)
    returned = lax.all_to_all(outbound, "attn", split_axis=0, concat_axis=0, tiled=True)
    summed = jnp.sum(
        returned.astype(jnp.float32).reshape(
            EXPERTS, attn_devices // EXPERTS, CAPACITY, model_width
        ),
        axis=1,
    )
    combined = jnp.dot(
        combiner, summed.reshape(EXPERTS * CAPACITY, model_width), precision=lax.Precision.HIGHEST
    )
    return (context, combined.astype(jnp.bfloat16))


def attention_rows(lengths, qs, nkf, nvf, keys, values, os, first, count):
    heads = qs.shape[1]
    width = keys.shape[2]
    kv = width // HEAD_DIM
    shared = heads // kv
    cached = keys.shape[1]
    scale = HEAD_DIM ** (-0.5)
    row_id = lax.broadcasted_iota(jnp.int32, (heads, HEAD_DIM), 0)
    mine = [(row_id >= g * shared) & (row_id < (g + 1) * shared) for g in range(kv)]
    lane = lax.broadcasted_iota(jnp.int32, (heads, cached), 1)

    def pick(parts):
        total = jnp.where(mine[0], parts[0], 0.0)
        for g in range(1, kv):
            total = jnp.where(mine[g], parts[g], total)
        return total

    for step in range(count):
        r = first + step
        q = qs[r]
        spread = jnp.concatenate([jnp.where(m, q, 0.0) for m in mine], axis=1).astype(jnp.bfloat16)
        s = lax.dot_general(
            spread, keys[r], (((1,), (1,)), ((), ())), preferred_element_type=jnp.float32
        ) * scale
        usable = lane < lengths[r]
        s = jnp.where(usable, s, -1e30)
        nk = nkf[pl.ds(r, 1), :]
        nv = nvf[pl.ds(r, 1), :]
        cut = [slice(g * HEAD_DIM, (g + 1) * HEAD_DIM) for g in range(kv)]
        own_key = pick([jnp.broadcast_to(nk[:, k], (heads, HEAD_DIM)) for k in cut])
        own_value = pick([jnp.broadcast_to(nv[:, k], (heads, HEAD_DIM)) for k in cut])
        own = jnp.sum(q * own_key, axis=1, keepdims=True) * scale
        highest = jnp.maximum(jnp.max(s, axis=1, keepdims=True), own)
        lifted = jnp.where(usable, jnp.exp(s - highest), 0.0)
        lifted_own = jnp.exp(own - highest)
        den = jnp.sum(lifted, axis=1, keepdims=True) + lifted_own
        w = (lifted / den).astype(jnp.bfloat16)
        w_own = (lifted_own / den).astype(jnp.bfloat16).astype(jnp.float32)
        o = jnp.dot(w, values[r], preferred_element_type=jnp.float32)
        os[r] = pick([o[:, k] for k in cut]) + w_own * own_value


def layer_kernel(
    attn_count,
    lengths,
    queries,
    new_keys,
    new_values,
    key_cache,
    value_cache,
    tokens,
    expert_ids,
    gate_weights,
    w_gate,
    w_up,
    w_down,
    context,
    expert_out,
    q_v, nk_v, nv_v, k_v, v_v, tok_v, ids_v, gw_v,
    qs, nkf, nvf, os, ctx_v,
    outbuf, near, far, x, hid, ring,
    psend, pgot, own_half, tf, tb, yb, zf, zb, home, comb_v, ob,
    in_sem, ring_sem, put_sem,
    d_s, d_r, fy_s, fy_r, fs_s, fs_r,
    p_s, p_r, y_s, y_r, h_s, h_r, o_s, o_r,
):
    group = attn_count // EXPERTS
    a = lax.axis_index("attn")
    c = lax.axis_index("exp")
    ex, j = a // group, a % group
    rows, width = tok_v.shape
    half = width // 2
    hidden = hid.shape[1]
    k_parts = width // DEPTH
    n_blocks = hidden // TILE
    out_blocks = half // TILE
    per_block = 2 * k_parts

    pairs = [
        (tokens, tok_v), (expert_ids, ids_v), (gate_weights, gw_v), (queries, q_v),
        (new_keys, nk_v), (new_values, nv_v), (key_cache, k_v), (value_cache, v_v),
    ]
    loads = [pltpu.make_async_copy(s, d, in_sem.at[n]) for n, (s, d) in enumerate(pairs)]
    for load in loads:
        load.start()

    def up_tile(n, k, w):
        t = n * per_block + k * 2 + w
        slot = t % RING
        source = w_up if w else w_gate
        return slot, pltpu.make_async_copy(
            source.at[pl.ds(k * DEPTH, DEPTH), pl.ds(pl.multiple_of(n * TILE, TILE), TILE)],
            ring.at[slot],
            ring_sem.at[slot],
        )

    def down_tile(i, own):
        t = n_blocks * per_block + i * 2 + own
        slot = t % RING
        side = c if own else 1 - c
        first = pl.multiple_of((side * out_blocks + i) * TILE, TILE)
        return slot, pltpu.make_async_copy(
            w_down.at[:, pl.ds(first, TILE)], ring.at[slot], ring_sem.at[slot]
        )

    ahead = RING // per_block

    def prefetch(n, carry):
        for k in range(k_parts):
            for w in range(2):
                up_tile(n, k, w)[1].start()
        return carry

    lax.fori_loop(0, ahead, prefetch, 0)

    z_peer = [((ex + d) % EXPERTS) * group + j for d in range(EXPERTS)]
    y_peer = [ex * group + (j + d) % group for d in range(group)]
    barrier = pltpu.get_barrier_semaphore()
    for peer in z_peer[1:] + y_peer[1:]:
        pl.semaphore_signal(barrier, inc=1, device_id={"attn": peer}, device_id_type=MESH)
    pl.semaphore_signal(barrier, inc=1, device_id={"exp": 1 - c}, device_id_type=MESH)

    for load in loads[:3]:
        load.wait()
    ids = ids_v[...]
    gates = gw_v[...]
    spots = EXPERTS * CAPACITY
    spot = lax.broadcasted_iota(jnp.int32, (spots, rows), 0)
    row_id = lax.broadcasted_iota(jnp.int32, (spots, rows), 1)
    first = ids[0:1, :] == spot // CAPACITY
    second = ids[1:2, :] == spot // CAPACITY
    routed = jnp.where(first | second, 1, 0)
    before = jnp.zeros((spots, rows), jnp.int32)
    for r in range(rows - 1):
        before = before + jnp.where(row_id > r, routed[:, r : r + 1], 0)
    chosen = (routed > 0) & (before == spot % CAPACITY)
    comb_v[...] = jnp.where(chosen, jnp.where(first, gates[0:1, :], gates[1:2, :]), 0.0)
    selector = jnp.where(chosen, 1.0, 0.0).astype(jnp.bfloat16)
    mine = tok_v[:, pl.ds(pl.multiple_of(c * half, half), half)]
    outgoing = jnp.dot(selector, mine, preferred_element_type=jnp.float32)
    outbuf[...] = outgoing.reshape(EXPERTS, CAPACITY, half).astype(jnp.bfloat16)
    pl.semaphore_wait(barrier, EXPERTS + group - 1)

    def remote(src, dst, s_sem, r_sem, device):
        return pltpu.make_async_remote_copy(
            src_ref=src, dst_ref=dst, send_sem=s_sem, recv_sem=r_sem,
            device_id=device, device_id_type=MESH,
        )

    sends = []
    for d in range(1, EXPERTS):
        e2 = (ex + d) % EXPERTS
        cp = remote(
            outbuf.at[e2], near.at[j * EXPERTS + ex], d_s.at[d], d_r.at[ex], {"attn": z_peer[d]}
        )
        cp.start()
        sends.append(cp)
    near[j * EXPERTS + ex] = outbuf[ex]

    for load in loads[3:]:
        load.wait()
    heads = qs.shape[1]
    for h in range(heads):
        qs[:, h, :] = q_v[:, h * HEAD_DIM : (h + 1) * HEAD_DIM].astype(jnp.float32)
    nkf[...] = nk_v[...].astype(jnp.float32)
    nvf[...] = nv_v[...].astype(jnp.float32)
    at_once = 4 if rows % 4 == 0 else 1

    def attend_some(n, carry):
        attention_rows(lengths, qs, nkf, nvf, k_v, v_v, os, n * at_once, at_once)
        return carry

    def pass_on(place, e, direct):
        if direct:
            for d in range(1, group):
                cp = remote(
                    near.at[place], near.at[place], fy_s.at[e, d], fy_r.at[place],
                    {"attn": y_peer[d]},
                )
                cp.start()
                sends.append(cp)
        cp = remote(near.at[place], far.at[place], fs_s.at[place], fs_r.at[place], {"exp": 1 - c})
        cp.start()
        sends.append(cp)

    pass_on(j * EXPERTS + ex, ex, True)
    third = rows // at_once // 3
    lax.fori_loop(0, third, attend_some, 0)
    for d in range(1, EXPERTS):
        e2 = (ex + EXPERTS - d) % EXPERTS
        place = j * EXPERTS + e2
        remote(near.at[place], near.at[place], d_s.at[d], d_r.at[e2], {"exp": 1 - c}).wait_recv()
        pass_on(place, e2, True)
    lax.fori_loop(third, 2 * third, attend_some, 0)
    for m in range(1, group):
        j2 = (j + m) % group
        for d in range(EXPERTS):
            e2 = (ex + EXPERTS - d) % EXPERTS
            place = j2 * EXPERTS + e2
            remote(
                near.at[place], near.at[place], fy_s.at[e2, m], fy_r.at[place], {"exp": 1 - c}
            ).wait_recv()
            pass_on(place, e2, False)
    lax.fori_loop(2 * third, rows // at_once, attend_some, 0)
    for place in range(attn_count):
        remote(
            near.at[place], far.at[place], fs_s.at[place], fs_r.at[place], {"exp": 1 - c}
        ).wait_recv()
    slots = attn_count * CAPACITY
    x[:, pl.ds(pl.multiple_of(c * half, half), half)] = (
        near[...].astype(jnp.float32).reshape(slots, half).astype(jnp.bfloat16)
    )
    x[:, pl.ds(pl.multiple_of((1 - c) * half, half), half)] = (
        far[...].astype(jnp.float32).reshape(slots, half).astype(jnp.bfloat16)
    )

    def hidden_block(n, carry):
        sums = [None, None]
        for k in range(k_parts):
            for w in range(2):
                slot, tile = up_tile(n, k, w)
                tile.wait()
                term = jnp.dot(
                    x[:, k * DEPTH : (k + 1) * DEPTH], ring[slot],
                    preferred_element_type=jnp.float32,
                )
                sums[w] = term if k == 0 else sums[w] + term

                @pl.when(n + ahead < n_blocks)
                def _():
                    up_tile(n + ahead, k, w)[1].start()

                later = (n + ahead - n_blocks) * k_parts + k

                @pl.when((n + ahead >= n_blocks) & (later < out_blocks))
                def _():
                    down_tile(later, w)[1].start()

        g, u = sums
        act = g / (1.0 + jnp.exp(-g)) * u
        hid[:, pl.ds(pl.multiple_of(n * TILE, TILE), TILE)] = act.astype(jnp.bfloat16)
        return carry

    lax.fori_loop(0, n_blocks, hidden_block, 0)

    def sibling(i):
        return remote(psend.at[i], pgot.at[i], p_s.at[i], p_r.at[i], {"exp": 1 - c})

    def across(i, d):
        j2 = (j + d) % group
        return remote(tb.at[i, j2], yb.at[i, j], y_s.at[i, d], y_r.at[i, j], {"attn": y_peer[d]})

    def to_home(i, d):
        e2 = (ex + d) % EXPERTS
        return remote(zb.at[i, e2], home.at[i, ex], h_s.at[i, d], h_r.at[i, ex], {"attn": z_peer[d]})

    def finish(i):
        total = zf[i]
        for d in range(1, group):
            j2 = (j + d) % group
            remote(
                tb.at[i, j2], yb.at[i, j2], y_s.at[i, d], y_r.at[i, j2], {"exp": 1 - c}
            ).wait_recv()
            total = total + yb[i, j2].astype(jnp.float32).reshape(EXPERTS * CAPACITY, TILE)
        zb[i] = total.reshape(EXPERTS, CAPACITY, TILE).astype(jnp.bfloat16)
        for d in range(1, EXPERTS):
            to_home(i, d).start()
        home[i, ex] = zb[i, ex]

    def merge(i):
        sibling(i).wait_recv()
        mine = own_half[i] + pgot[i]
        tf[...] = mine.reshape(group, EXPERTS * CAPACITY, TILE)
        tb[i] = mine.reshape(group, EXPERTS, CAPACITY, TILE).astype(jnp.bfloat16)
        zf[i] = tf[j]
        for d in range(1, group):
            across(i, d).start()

    def down_block(i, carry):
        slot, tile = down_tile(i, 0)
        tile.wait()
        psend[i] = jnp.dot(hid[...], ring[slot], preferred_element_type=jnp.float32)
        sibling(i).start()
        slot, tile = down_tile(i, 1)
        tile.wait()
        own_half[i] = jnp.dot(hid[...], ring[slot], preferred_element_type=jnp.float32)

        @pl.when(i >= 1)
        def _():
            merge(i - 1)

        @pl.when(i >= LAG)
        def _():
            finish(i - LAG)

        return carry

    lax.fori_loop(0, out_blocks, down_block, 0)
    merge(out_blocks - 1)
    for h in range(heads):
        ctx_v[:, h * HEAD_DIM : (h + 1) * HEAD_DIM] = os[:, h, :].astype(jnp.bfloat16)
    put_context = pltpu.make_async_copy(ctx_v, context, put_sem.at[0])
    put_context.start()

    def finish_rest(i, carry):
        finish(i)
        return carry

    lax.fori_loop(max(out_blocks - LAG, 0), out_blocks, finish_rest, 0)

    def combine(i, carry):
        for d in range(1, EXPERTS):
            e2 = (ex + d) % EXPERTS
            remote(
                zb.at[i, e2], home.at[i, e2], h_s.at[i, d], h_r.at[i, e2], {"exp": 1 - c}
            ).wait_recv()
        ob[:, pl.ds(pl.multiple_of(i * TILE, TILE), TILE)] = lax.dot_general(
            comb_v[...], home[i].astype(jnp.float32).reshape(spots, TILE),
            (((0,), (0,)), ((), ())), precision=lax.Precision.HIGHEST, preferred_element_type=jnp.float32,
        ).astype(jnp.bfloat16)
        return carry

    lax.fori_loop(0, out_blocks, combine, 0)
    own_columns = pl.ds(pl.multiple_of(c * half, half), half)
    give = remote(ob, expert_out.at[:, own_columns], o_s, o_r, {"exp": 1 - c})
    give.start()
    put_out = pltpu.make_async_copy(ob, expert_out.at[:, own_columns], put_sem.at[1])
    put_out.start()
    for cp in sends:
        cp.wait_send()

    def drain(i, carry):
        sibling(i).wait_send()
        for d in range(1, group):
            across(i, d).wait_send()
        for d in range(1, EXPERTS):
            to_home(i, d).wait_send()
        return carry

    lax.fori_loop(0, out_blocks, drain, 0)
    put_context.wait()
    put_out.wait()
    other_columns = pl.ds(pl.multiple_of((1 - c) * half, half), half)
    give.wait_send()
    remote(ob, expert_out.at[:, other_columns], o_s, o_r, {"exp": 1 - c}).wait_recv()


def fused(
    queries, new_keys, new_values, key_cache, value_cache, cache_lengths,
    tokens, expert_ids, gate_weights, w_gate, w_up, w_down,
):
    n = lax.axis_size("attn")
    group = n // EXPERTS
    rows, width = tokens.shape
    half = width // 2
    heads = queries.shape[1] // HEAD_DIM
    hidden = w_gate.shape[1]
    blocks = half // TILE
    slots = n * CAPACITY
    bf, f32 = jnp.bfloat16, jnp.float32
    vm, dma = pltpu.VMEM, pltpu.SemaphoreType.DMA
    anywhere = pl.BlockSpec(memory_space=pl.ANY)
    return pl.pallas_call(
        functools.partial(layer_kernel, n),
        out_shape=(
            jax.ShapeDtypeStruct(queries.shape, bf),
            jax.ShapeDtypeStruct(tokens.shape, bf),
        ),
        in_specs=[pl.BlockSpec(memory_space=pltpu.SMEM)] + [anywhere] * 11,
        out_specs=(anywhere, anywhere),
        scratch_shapes=[
            vm(queries.shape, bf), vm(new_keys.shape, bf), vm(new_values.shape, bf),
            vm(key_cache.shape, bf), vm(value_cache.shape, bf), vm(tokens.shape, bf),
            vm((2, rows), jnp.int32), vm((2, rows), f32),
            vm((rows, heads, HEAD_DIM), f32), vm(new_keys.shape, f32), vm(new_values.shape, f32),
            vm((rows, heads, HEAD_DIM), f32), vm(queries.shape, bf),
            vm((EXPERTS, CAPACITY, half), bf), vm((n, CAPACITY, half), bf),
            vm((n, CAPACITY, half), bf), vm((slots, width), bf), vm((slots, hidden), bf),
            vm((RING, DEPTH, TILE), bf),
            vm((blocks, slots, TILE), f32), vm((blocks, slots, TILE), f32),
            vm((blocks, slots, TILE), f32),
            vm((group, EXPERTS * CAPACITY, TILE), f32),
            vm((blocks, group, EXPERTS, CAPACITY, TILE), bf),
            vm((blocks, group, EXPERTS, CAPACITY, TILE), bf),
            vm((blocks, EXPERTS * CAPACITY, TILE), f32),
            vm((blocks, EXPERTS, CAPACITY, TILE), bf), vm((blocks, EXPERTS, CAPACITY, TILE), bf),
            vm((EXPERTS * CAPACITY, rows), f32), vm((rows, half), bf),
            dma((8,)), dma((RING,)), dma((2,)),
            dma((EXPERTS,)), dma((EXPERTS,)), dma((EXPERTS, group)), dma((n,)), dma((n,)), dma((n,)),
            dma((blocks,)), dma((blocks,)), dma((blocks, group)), dma((blocks, group)),
            dma((blocks, EXPERTS)), dma((blocks, EXPERTS)), dma(()), dma(()),
        ],
        compiler_params=pltpu.CompilerParams(
            collective_id=0, has_side_effects=True, vmem_limit_bytes=60 * 1024 * 1024
        ),
        name="decode_layer",
    )(
        cache_lengths, queries, new_keys, new_values, key_cache, value_cache,
        tokens, expert_ids.T, gate_weights.T, w_gate, w_up, w_down,
    )


def fits(mesh):
    return mesh.shape["exp"] == 2 and mesh.shape["attn"] == 2 * EXPERTS


def solution(mesh):
    placed = (
        P(("groups", "attn"), "exp"),
        P(("groups", "attn"), "exp"),
        P(("groups", "attn"), "exp"),
        P(("groups", "attn"), None, "exp"),
        P(("groups", "attn"), None, "exp"),
        P(("groups", "attn")),
        P(("groups", "attn"), None),
        P(("groups", "attn"), None),
        P(("groups", "attn"), None),
        P(None, ("attn", "exp")),
        P(None, ("attn", "exp")),
        P(("attn", "exp"), None),
    )
    return jax.shard_map(
        fused if fits(mesh) else per_device,
        mesh=mesh,
        in_specs=placed,
        out_specs=(P(("groups", "attn"), "exp"), P(("groups", "attn"), None)),
        check_vma=False,
    )
```
